32 devices in a mesh: strip: 4 (over y, core), wide: 4 (over z), comp: 2 (over x).
Axes of the slice: x: 2, y: 2, z: 4, core: 2. Of those that a mesh axis runs over, the one named last changes fastest.
Arguments:
- spectrum: bfloat16 [1152, 49152], P('comp', ('strip', 'wide')), may hold values from 0.049804688 to 2
- wet_mask: int32 [192, 256], P('strip'), may hold values 0 or 1
- currents: float32 [2, 32, 16], P(None, 'strip', 'wide'), may hold values from -3 to 3
- remap_index: int32 [4, 49152], P(None, 'strip'), may hold values from 0 to 127, as said below
- remap_weights: float32 [4, 49152], P(None, 'strip'), may hold values from 0.2 to 0.6
- source_matrix: bfloat16 [1152, 1152], P('comp'), may hold values from -0.1875 to 0.1875
Outputs:
- updated: bfloat16 [1152, 49152], P('comp', ('strip', 'wide'))
- stokes: float32 [2, 32, 49152], P(None, 'comp', ('strip', 'wide'))
The draws below stay inside these ranges and needn't reach their ends.
Inputs may be any that keep to these rules, and one draw needn't show every extreme that they name: `remap_index`: a point's cells lie in the ocean rows and columns of its strip next to the point's own location.
All inputs are finite; a program needn't handle non-finite values. No bound on the sum of `wet_mask` on one device may be relied on, other than what follows from the above.
Results may differ from the reference program's by a relative error of at most 0.0048.
Values may be sent and summed in bfloat16 or wider, within the bound.
A program may use at most 128 MiB of HBM per device.

```python
import math
import jax
import jax.numpy as jnp
from jax import lax

NFREQ = 32
NDIR = 36
LEVELS = 32
LON = 256
SUBSTEPS = 4
LAT_DEV = 48
OLAT_DEV = 8
NBIN = 1152
LAT = 192
NPTS = 49152
OLAT = 32
OLON = 16
N_STRIP = 4


def draw_remap_index(key, part):
    point = jnp.arange(NPTS, dtype=jnp.int32) % (LAT_DEV * LON)
    row = point // LON
    column = point % LON
    span = OLON // LON + 1
    key_row = jax.random.fold_in(key, 11)
    key_column = jax.random.fold_in(key, 23)
    row_shift = jax.random.randint(key_row, (NPTS,), -1, 1, dtype=jnp.int32)
    column_shift = jax.random.randint(key_column, (NPTS,), -1, span, dtype=jnp.int32)
    base_row = jnp.clip(row * OLAT_DEV // LAT_DEV + row_shift, 0, OLAT_DEV - 1)
    base_column = column * OLON // LON + column_shift
    corner = jnp.arange(4, dtype=jnp.int32)
    rows = jnp.minimum(base_row[None, :] + (corner // 2)[:, None], OLAT_DEV - 1)
    columns = (base_column[None, :] + (corner % 2)[:, None] + OLON) % OLON
    return (rows * OLON + columns).astype(jnp.int32)


def set_ends(result, key, least, high):
    longest = result.shape.index(max(result.shape))
    spots = []
    for shift in (0, 1):
        where = [jax.random.randint(jax.random.fold_in(key, axis), (), 0, length) for axis, length in enumerate(result.shape)]
        where[longest] = (where[longest] + shift) % result.shape[longest]
        spots.append(tuple(where))
    return result.at[spots[0]].set(least).at[spots[1]].set(high)


def levels(rng, dims, split, low, top_value):
    loudness, own = 1.0, jax.random.fold_in(rng, 6)
    for dim, shards_of in split:
        heights = jnp.exp(jax.random.uniform(jax.random.fold_in(own, dim), (shards_of,), jnp.float32, low / len(split), top_value / len(split)))
        loudness = loudness * jnp.repeat(heights, dims[dim] // shards_of).reshape([-1 if axis == dim else 1 for axis in range(len(dims))])
    return loudness


def centred(stream_key, extent, scale, most, shards=(), kind=jnp.bfloat16):
    result = scale * jax.random.normal(stream_key, extent, jnp.float32)
    if shards:
        result = result * levels(stream_key, extent, shards, -0.22, 0.18)
    return jnp.clip(result, -most, most).astype(kind)


def setup_inputs(seed: int = 0) -> dict:
    arg_keys = jax.random.split(jax.random.key(seed), 7)
    return {
        "spectrum": jnp.clip(jnp.exp(math.log(2.0) - 3.6927934 * jax.random.uniform(arg_keys[0], (NBIN, NPTS), jnp.float32) ** levels(arg_keys[0], (NBIN, NPTS), ((0, 2), (1, 16)), -0.2, 0.2)), 0.049804688, 2.0).astype(jnp.bfloat16),
        "wet_mask": set_ends((jax.random.randint(arg_keys[1], (LAT, LON), 0, 8) < 7).astype(jnp.int32), jax.random.fold_in(arg_keys[1], 1), 0, 1),
        "currents": centred(arg_keys[2], (2, OLAT, OLON), 0.3, 3.0, ((1, 4), (2, 4)), jnp.float32),
        "remap_index": draw_remap_index(jax.random.fold_in(arg_keys[6], 71), 0),
        "remap_weights": jnp.clip(0.2 + 0.400000021 * jax.random.uniform(arg_keys[4], (4, NPTS), jnp.float32) ** levels(arg_keys[4], (4, NPTS), ((1, 4),), -0.2, 0.2), 0.2, 0.6),
        "source_matrix": centred(arg_keys[5], (NBIN, NBIN), NBIN ** -0.5, 0.1875, ((0, 2),)),
    }


courant = 0.45

def bin_speeds(first_bin, bin_count):
    index = first_bin + jnp.arange(bin_count, dtype=jnp.int32)
    freq_index = (index // NDIR).astype(jnp.float32)
    dir_index = (index % NDIR).astype(jnp.float32)
    group_speed = 0.35 + 0.65 * (NFREQ - 1 - freq_index) / (NFREQ - 1)
    heading = 2.0 * math.pi * (dir_index + 0.5) / NDIR
    return ((group_speed * jnp.cos(heading))[:, None, None], (group_speed * jnp.sin(heading))[:, None, None])

def stokes_kernel(first_bin, bin_count, first_level, level_count):
    index = first_bin + jnp.arange(bin_count, dtype=jnp.int32)
    frequency = (index // NDIR + 1).astype(jnp.float32)
    heading = 2.0 * math.pi * ((index % NDIR).astype(jnp.float32) + 0.5) / NDIR
    level_index = (first_level + jnp.arange(level_count, dtype=jnp.int32)).astype(jnp.float32)
    damping = jnp.exp(-4.0 * frequency[None, :] * (level_index[:, None] + 0.5) / (NFREQ * LEVELS))
    amplitude = damping * (frequency / NFREQ)[None, :] / math.sqrt(NDIR)
    eastward = amplitude * jnp.cos(heading)[None, :]
    northward = amplitude * jnp.sin(heading)[None, :]
    return jnp.concatenate([eastward, northward], 0).astype(jnp.bfloat16)

def substep(energy, east_flow, north_flow, wet_frac, speed_east, speed_north):
    east_speed = speed_east + east_flow[None]
    north_speed = speed_north + north_flow[None]
    flux_lon = jnp.maximum(east_speed, 0.0) * energy + jnp.minimum(jnp.roll(east_speed, -1, 2), 0.0) * jnp.roll(energy, -1, 2)
    flux_lat = jnp.maximum(north_speed[:, :-1], 0.0) * energy[:, :-1] + jnp.minimum(north_speed[:, 1:], 0.0) * energy[:, 1:]
    spread = flux_lon - jnp.roll(flux_lon, 1, 2)
    change = spread[:, 1:-1] + flux_lat[:, 1:] - flux_lat[:, :-1]
    return wet_frac[1:-1] * (energy[:, 1:-1] - courant * change)

def reference(spectrum, wet_mask, currents, remap_index, remap_weights, source_matrix):
    strip_points = LAT_DEV * LON
    ocean_flow = currents.reshape(2, N_STRIP, OLAT_DEV * OLON)
    cell_index = remap_index.reshape(4, N_STRIP, strip_points)
    strip_ids = jnp.arange(N_STRIP, dtype=jnp.int32)[None, :, None]
    picked = ocean_flow[:, strip_ids, cell_index]
    shares = remap_weights.reshape(4, N_STRIP, strip_points)
    surface = lax.optimization_barrier(jnp.sum(picked * shares[None], 1)).reshape(2, LAT, LON)
    wet_frac = wet_mask.astype(jnp.float32)
    padded = jnp.pad(jnp.concatenate([surface, wet_frac[None]], 0), ((0, 0), (1, 1), (0, 0)))
    speed_east, speed_north = bin_speeds(0, NBIN)
    speed_east = speed_east.reshape(NFREQ, NDIR, 1, 1)
    speed_north = speed_north.reshape(NFREQ, NDIR, 1, 1)
    energy = spectrum.astype(jnp.float32).reshape(NFREQ, NDIR, LAT, LON) * wet_frac

    def advect_block(inputs):
        block_energy, block_east, block_north = inputs
        for repeat in range(SUBSTEPS):
            widened = jnp.pad(block_energy, ((0, 0), (1, 1), (0, 0)))
            block_energy = substep(widened, padded[0], padded[1], padded[2], block_east, block_north)
        return block_energy.astype(jnp.bfloat16)
    propagated = lax.map(advect_block, (energy, speed_east, speed_north)).reshape(NBIN, NPTS)
    source = jnp.dot(source_matrix, propagated, preferred_element_type=jnp.float32)
    wet_flat = wet_frac.reshape(-1)
    updated = (wet_flat[None, :] * jnp.maximum(propagated.astype(jnp.float32) + source, 0.0)).astype(jnp.bfloat16)
    kernel = stokes_kernel(0, NBIN, 0, LEVELS)
    stokes = jnp.dot(kernel, propagated, preferred_element_type=jnp.float32).reshape(2, LEVELS, NPTS)
    return (updated, stokes)
```

```python
import functools
import math

import jax
import jax.numpy as jnp
import numpy as np
from jax import lax
from jax.experimental import pallas as pl
from jax.experimental.pallas import tpu as pltpu
from jax.sharding import PartitionSpec as P

NFREQ = 32
NDIR = 36
LEVELS = 32
SUBSTEPS = 4


courant = 0.45


def extended(cells, sides, width):
    for axis, dim in sides:
        count = lax.axis_size(axis)
        ends = count - 1
        head = lax.slice_in_dim(cells, 0, width, axis=dim)
        tail = lax.slice_in_dim(cells, cells.shape[dim] - width, cells.shape[dim], axis=dim)
        cells = jnp.concatenate(
            [
                lax.ppermute(tail, axis, [(i, (i + 1) % count) for i in range(ends)]),
                cells,
                lax.ppermute(head, axis, [((i + 1) % count, i) for i in range(ends)]),
            ],
            axis=dim,
        )
    return cells


def bin_speeds(first_bin, bin_count):
    index = first_bin + jnp.arange(bin_count, dtype=jnp.int32)
    freq_index = (index // NDIR).astype(jnp.float32)
    dir_index = (index % NDIR).astype(jnp.float32)
    group_speed = 0.35 + 0.65 * (NFREQ - 1 - freq_index) / (NFREQ - 1)
    heading = 2.0 * math.pi * (dir_index + 0.5) / NDIR
    return (
        (group_speed * jnp.cos(heading))[:, None, None],
        (group_speed * jnp.sin(heading))[:, None, None],
    )


def stokes_kernel(bin_count, first_level, level_count):
    index = jnp.arange(bin_count, dtype=jnp.int32)
    frequency = (index // NDIR + 1).astype(jnp.float32)
    heading = 2.0 * math.pi * ((index % NDIR).astype(jnp.float32) + 0.5) / NDIR
    level_index = (first_level + jnp.arange(level_count, dtype=jnp.int32)).astype(jnp.float32)
    damping = jnp.exp(-4.0 * frequency[None, :] * (level_index[:, None] + 0.5) / (NFREQ * LEVELS))
    amplitude = damping * (frequency / NFREQ)[None, :] / math.sqrt(NDIR)
    eastward = amplitude * jnp.cos(heading)[None, :]
    northward = amplitude * jnp.sin(heading)[None, :]
    return jnp.concatenate([eastward, northward], 0).astype(jnp.bfloat16)


def substep(energy, east_flow, north_flow, wet_frac, speed_east, speed_north):
    east_speed = speed_east + east_flow[None]
    north_speed = speed_north + north_flow[None]
    flux_lon = jnp.maximum(east_speed, 0.0) * energy + jnp.minimum(
        jnp.roll(east_speed, -1, 2), 0.0
    ) * jnp.roll(energy, -1, 2)
    flux_lat = (
        jnp.maximum(north_speed[:, :-1], 0.0) * energy[:, :-1]
        + jnp.minimum(north_speed[:, 1:], 0.0) * energy[:, 1:]
    )
    spread = flux_lon - jnp.roll(flux_lon, 1, 2)
    change = spread[:, 1:-1] + flux_lat[:, 1:] - flux_lat[:, :-1]
    return wet_frac[1:-1] * (energy[:, 1:-1] - courant * change)


def advance(widened, speed_east, speed_north):
    bin_share = speed_east.shape[0]
    energy = widened[:bin_share]
    east_flow = widened[bin_share]
    north_flow = widened[bin_share + 1]
    wet_frac = widened[bin_share + 2]
    energy = substep(energy, east_flow, north_flow, wet_frac, speed_east, speed_north)
    return energy


def interpolate(tiles, remap_index, remap_weights, lat_rows, lon_cells):
    ocean_rows = tiles.shape[1]
    ocean_cols = tiles.shape[2]
    block_points = 4 * lon_cells
    block_count = lat_rows // 4
    flow_table = tiles.reshape(2 * ocean_rows, ocean_cols)
    index_blocks = jnp.transpose(remap_index.reshape(4, block_count, block_points), (1, 0, 2))
    weight_blocks = jnp.transpose(remap_weights.reshape(4, block_count, block_points), (1, 0, 2))
    column_ids = jnp.arange(ocean_cols, dtype=jnp.int32)[None, :, None]
    row_ids = jnp.arange(ocean_rows, dtype=jnp.int32)[None, :, None]

    def one_block(inputs):
        cells, shares = inputs
        column_of = cells % ocean_cols
        row_of = cells // ocean_cols
        column_hot = (column_of[:, None, :] == column_ids).astype(jnp.float32)
        picked = jnp.einsum("mk,jkp->jmp", flow_table, column_hot, precision=lax.Precision.HIGHEST)
        picked = picked.reshape(4, 2, ocean_rows, block_points)
        row_weight = (row_of[:, None, :] == row_ids).astype(jnp.float32) * shares[:, None, :]
        return jnp.sum(picked * row_weight[:, None], (0, 2))

    blocks = lax.map(one_block, (index_blocks, weight_blocks))
    return jnp.transpose(blocks, (1, 0, 2)).reshape(2, lat_rows, lon_cells)


def plain_device(spectrum, wet_mask, currents, remap_index, remap_weights, source_matrix):
    wide_count = lax.axis_size("wide")
    wide_index = lax.axis_index("wide")
    comp_index = lax.axis_index("comp")
    lat_rows, lon_cells = wet_mask.shape
    local_bins, points = spectrum.shape
    tiles = lax.all_gather(currents, "wide", axis=2, tiled=True)
    surface = interpolate(tiles, remap_index, remap_weights, lat_rows, lon_cells)
    wet_frac = wet_mask.astype(jnp.float32)
    row_count = lat_rows // wide_count
    wet_rows = lax.dynamic_slice_in_dim(wet_frac, wide_index * row_count, row_count, 0)
    flow_rows = lax.dynamic_slice_in_dim(surface, wide_index * row_count, row_count, 1)
    speed_east, speed_north = bin_speeds(comp_index * local_bins, local_bins)
    energy = spectrum.astype(jnp.float32).reshape(local_bins, row_count, lon_cells) * wet_rows
    for repeat in range(SUBSTEPS):
        fields = jnp.concatenate([energy, flow_rows, wet_rows[None]], 0)
        widened = extended(fields, ((("strip", "wide"), 1),), 1)
        energy = advance(widened, speed_east, speed_north)
    returned = energy.astype(jnp.bfloat16).reshape(local_bins, points)
    level_rows = LEVELS // lax.axis_size("comp")
    first_level = comp_index * level_rows
    fragment = lax.all_gather(returned, "comp", axis=0, tiled=True)
    width = fragment.shape[0]
    kernel = stokes_kernel(width, first_level, level_rows)
    source_part = jnp.dot(source_matrix, fragment, preferred_element_type=jnp.float32)
    drift_part = jnp.dot(kernel, fragment, preferred_element_type=jnp.float32)
    wet_points = lax.dynamic_slice_in_dim(wet_frac.reshape(-1), wide_index * points, points, 0)
    updated = (
        wet_points[None, :] * jnp.maximum(returned.astype(jnp.float32) + source_part, 0.0)
    ).astype(jnp.bfloat16)
    return (updated, drift_part.reshape(2, level_rows, points))


CHUNK = 32
BLOCK = 16
AHEAD = 4
TILE = 512
GROUP = 256
MESH = pl.DeviceIdType.MESH


def speed_table(bin_count, bins_total):
    index = np.arange(bins_total)
    group_speed = 0.35 + 0.65 * (NFREQ - 1 - index // NDIR) / (NFREQ - 1)
    heading = 2.0 * math.pi * (index % NDIR + 0.5) / NDIR
    both = courant * np.stack([group_speed * np.cos(heading), group_speed * np.sin(heading)])
    return np.ascontiguousarray(np.broadcast_to(both[:, :, None], (2, bins_total, 128)).astype(np.float32))


def drift_table(bins_total, comp_count):
    index = np.arange(bins_total)
    frequency = (index // NDIR + 1).astype(np.float32)
    heading = 2.0 * math.pi * (index % NDIR + 0.5) / NDIR
    level = np.arange(LEVELS, dtype=np.float32)
    damping = np.exp(-4.0 * frequency[None, :] * (level[:, None] + 0.5) / (NFREQ * LEVELS))
    amplitude = damping * (frequency / NFREQ)[None, :] / math.sqrt(NDIR)
    both = np.stack([amplitude * np.cos(heading), amplitude * np.sin(heading)])
    both = both.reshape(2, comp_count, LEVELS // comp_count, bins_total)
    both = np.transpose(both, (1, 0, 2, 3)).reshape(comp_count, -1, bins_total)
    return both.astype(np.float32).astype(jnp.bfloat16)


def wave_kernel(
    sizes, spec, mask, cur, idx, wgt, src, speed, drift,
    upd, stk,
    spec_v, top, bot, prop, other, acc, src_v, parts, speed_v, idx_v, wgt_v,
    flow, cur_pad, cur_flat, curs, state, coef,
    load_sem, spec_sem, up_send, down_send, bot_recv, top_recv,
    cur_send, cur_recv, edge_send, edge_recv, prop_send, prop_recv, out_sem,
):
    ns, nw, nc, rows, lon = sizes
    bins, points = spec.shape
    depth = SUBSTEPS
    wide_lanes = depth * lon
    chunks = bins // CHUNK
    drift_rows = drift.shape[1]
    ocean_rows, ocean_cols = cur.shape[1], cur.shape[2]
    s, w, c = lax.axis_index("strip"), lax.axis_index("wide"), lax.axis_index("comp")
    place = s * nw + w
    has_prev = place > 0
    has_next = place < ns * nw - 1
    before = jnp.maximum(place - 1, 0)
    after = jnp.minimum(place + 1, ns * nw - 1)
    prev_dev = (before // nw, before % nw, c)
    next_dev = (after // nw, after % nw, c)
    partner = (s, w, 1 - c)

    def span(k):
        return pl.ds(pl.multiple_of(k * CHUNK, CHUNK), CHUNK)

    own_rows = pl.ds(pl.multiple_of(c * bins, BLOCK), bins)
    own_points = pl.ds(pl.multiple_of(w * points, 128), points)
    loads = [
        pltpu.make_async_copy(idx.at[:, own_points], idx_v, load_sem.at[0]),
        pltpu.make_async_copy(wgt.at[:, own_points], wgt_v, load_sem.at[1]),
        pltpu.make_async_copy(speed.at[:, own_rows, :], speed_v, load_sem.at[2]),
        pltpu.make_async_copy(src, src_v.at[pl.ds(0, bins), :], load_sem.at[3]),
        pltpu.make_async_copy(drift.at[c], src_v.at[pl.ds(bins, drift_rows), :], load_sem.at[4]),
    ]

    def load_chunk(k):
        return pltpu.make_async_copy(spec.at[span(k), :], spec_v.at[span(k), :], spec_sem.at[k])

    def send_up(k):
        return pltpu.make_async_remote_copy(
            src_ref=spec.at[span(k), pl.ds(0, wide_lanes)], dst_ref=bot.at[span(k), :],
            send_sem=up_send.at[k], recv_sem=bot_recv.at[k], device_id=prev_dev, device_id_type=MESH)

    def send_down(k):
        return pltpu.make_async_remote_copy(
            src_ref=spec.at[span(k), pl.ds(points - wide_lanes, wide_lanes)], dst_ref=top.at[span(k), :],
            send_sem=down_send.at[k], recv_sem=top_recv.at[k], device_id=next_dev, device_id_type=MESH)

    def send_cur(step):
        return pltpu.make_async_remote_copy(
            src_ref=cur_flat, dst_ref=curs.at[w], send_sem=cur_send.at[step], recv_sem=cur_recv.at[step],
            device_id=(s, (w + step + 1) % nw, c), device_id_type=MESH)

    def take_cur(step):
        return pltpu.make_async_remote_copy(
            src_ref=cur_flat, dst_ref=curs.at[(w + nw - step - 1) % nw], send_sem=cur_send.at[step],
            recv_sem=cur_recv.at[step], device_id=(s, (w + step + 1) % nw, c), device_id_type=MESH)

    def send_edge(up):
        if up:
            return pltpu.make_async_remote_copy(
                src_ref=flow.at[:, pl.ds(wide_lanes, wide_lanes)],
                dst_ref=flow.at[:, pl.ds(wide_lanes + points, wide_lanes)],
                send_sem=edge_send.at[0], recv_sem=edge_recv.at[0], device_id=prev_dev, device_id_type=MESH)
        return pltpu.make_async_remote_copy(
            src_ref=flow.at[:, pl.ds(points, wide_lanes)], dst_ref=flow.at[:, pl.ds(0, wide_lanes)],
            send_sem=edge_send.at[1], recv_sem=edge_recv.at[1], device_id=next_dev, device_id_type=MESH)

    def send_prop(k):
        return pltpu.make_async_remote_copy(
            src_ref=prop.at[span(k), :], dst_ref=other.at[span(k), :],
            send_sem=prop_send.at[k], recv_sem=prop_recv.at[k], device_id=partner, device_id_type=MESH)

    for copy in loads:
        copy.start()

    @pl.loop(0, chunks)
    def _(k):
        load_chunk(k).start()

    flow[...] = jnp.zeros_like(flow)

    @pl.when(jnp.logical_not(has_prev))
    def _():
        top[...] = jnp.zeros_like(top)

    @pl.when(jnp.logical_not(has_next))
    def _():
        bot[...] = jnp.zeros_like(bot)

    barrier = pltpu.get_barrier_semaphore()
    for step in range(1, nw):
        pl.semaphore_signal(barrier, inc=1, device_id=(s, (w + step) % nw, c), device_id_type=MESH)
    pl.semaphore_signal(barrier, inc=1, device_id=partner, device_id_type=MESH)
    cross_prev = jnp.logical_and(has_prev, w == 0)
    cross_next = jnp.logical_and(has_next, w == nw - 1)

    @pl.when(cross_prev)
    def _():
        pl.semaphore_signal(barrier, inc=1, device_id=prev_dev, device_id_type=MESH)

    @pl.when(cross_next)
    def _():
        pl.semaphore_signal(barrier, inc=1, device_id=next_dev, device_id_type=MESH)

    cur_pad[...] = jnp.zeros_like(cur_pad)
    cur_flat[...] = jnp.zeros_like(cur_flat)
    for comp in range(2):
        cur_pad[comp, 0:ocean_rows, 0:ocean_cols] = cur[comp]
        line = cur_pad[comp, 0:1, :]
        for row in range(1, ocean_rows):
            line = line + pltpu.roll(cur_pad[comp, row:row + 1, :], row * ocean_cols, 1)
        cur_flat[comp:comp + 1, :] = line
    curs[w] = cur_flat[...]

    pl.semaphore_wait(barrier, nw + cross_prev.astype(jnp.int32) + cross_next.astype(jnp.int32))

    for step in range(nw - 1):
        send_cur(step).start()

    def start_halo(k):
        @pl.when(has_prev)
        def _():
            send_up(k).start()

        @pl.when(has_next)
        def _():
            send_down(k).start()

    @pl.loop(0, AHEAD)
    def _(k):
        start_halo(k)

    for row in range(rows):
        lanes = slice(wide_lanes + row * lon, wide_lanes + (row + 1) * lon)
        flow[2:3, lanes] = mask[pl.ds(w * rows + row, 1), :].astype(jnp.float32)
    for copy in loads[:2]:
        copy.wait()
    for step in range(nw - 1):
        take_cur(step).wait_recv()
    total_cols = ocean_cols * nw
    for piece in range(points // 256):
        lanes = [slice(piece * 256 + h * 128, piece * 256 + (h + 1) * 128) for h in range(2)]
        cells = jnp.concatenate([idx_v[:, part] for part in lanes], 0)
        shares = jnp.concatenate([wgt_v[:, part] for part in lanes], 0)
        row_of, col_of = cells // total_cols, cells % total_cols
        tile_of = col_of // ocean_cols
        spot = row_of * ocean_cols + col_of % ocean_cols
        for comp in range(2):
            picked = jnp.zeros(cells.shape, jnp.float32)
            for tile in range(nw):
                table = jnp.broadcast_to(curs[tile, comp:comp + 1, :], cells.shape)
                found = jnp.take_along_axis(table, spot, axis=1, mode="promise_in_bounds")
                picked = jnp.where(tile_of == tile, found, picked)
            picked = courant * picked * shares
            for h in range(2):
                flow[comp:comp + 1, wide_lanes + piece * 256 + h * 128:wide_lanes + piece * 256 + (h + 1) * 128] = (
                    jnp.sum(picked[4 * h:4 * h + 4], 0, keepdims=True))

    @pl.when(has_prev)
    def _():
        send_edge(True).start()

    @pl.when(has_next)
    def _():
        send_edge(False).start()

    for copy in loads[2:]:
        copy.wait()
    for half in range(nc):
        parts[half] = src_v[:, half * bins:(half + 1) * bins]

    @pl.when(has_next)
    def _():
        send_edge(True).wait_recv()

    @pl.when(has_prev)
    def _():
        send_edge(False).wait_recv()

    ext = rows + 2 * depth

    def at(row):
        return slice(row * lon, (row + 1) * lon)

    def block(first):
        here = pl.ds(pl.multiple_of(first, BLOCK), BLOCK)
        cx = jnp.concatenate([speed_v[0, here, :]] * (lon // 128), 1)
        cy = jnp.concatenate([speed_v[1, here, :]] * (lon // 128), 1)
        for row in range(ext):
            if row < depth:
                cells = top[here, at(row)]
            elif row < depth + rows:
                cells = spec_v[here, at(row - depth)]
            else:
                cells = bot[here, at(row - depth - rows)]
            state[0, :, at(row)] = cells.astype(jnp.float32) * flow[2:3, at(row)]

        def north(row):
            speed_n = cy + flow[1:2, at(row)]
            up = jnp.maximum(speed_n, 0.0)
            return up, up - speed_n

        below, mid = north(0), north(1)
        for row in range(1, ext - 1):
            above = north(row + 1)
            speed_e = cx + flow[0:1, at(row)]
            east = jnp.maximum(speed_e, 0.0)
            west = east - speed_e
            wet = flow[2:3, at(row)]
            coef[0, :, at(row)] = wet * (1.0 - (east + west) - (mid[0] + mid[1]))
            coef[1, :, at(row)] = wet * pltpu.roll(east, 1, 1)
            coef[2, :, at(row)] = wet * pltpu.roll(west, lon - 1, 1)
            coef[3, :, at(row)] = wet * below[0]
            coef[4, :, at(row)] = wet * above[1]
            below, mid = mid, above
        for repeat in range(depth):
            now, later = repeat % 2, (repeat + 1) % 2
            low, mid_e = state[now, :, at(repeat)], state[now, :, at(repeat + 1)]
            for row in range(repeat + 1, ext - 1 - repeat):
                high = state[now, :, at(row + 1)]
                result = (
                    (coef[0, :, at(row)] * mid_e
                     + (coef[1, :, at(row)] * pltpu.roll(mid_e, 1, 1)
                        + coef[2, :, at(row)] * pltpu.roll(mid_e, lon - 1, 1)))
                    + (coef[3, :, at(row)] * low + coef[4, :, at(row)] * high))
                if repeat < depth - 1:
                    state[later, :, at(row)] = result
                else:
                    prop[here, at(row - depth)] = result.astype(jnp.bfloat16)
                low, mid_e = mid_e, high

    @pl.loop(0, chunks)
    def _(k):
        load_chunk(k).wait()

        @pl.when(has_next)
        def _():
            send_up(k).wait_recv()

        @pl.when(has_prev)
        def _():
            send_down(k).wait_recv()

        @pl.when(k + AHEAD < chunks)
        def _():
            start_halo(k + AHEAD)

        @pl.loop(0, CHUNK // BLOCK)
        def _(j):
            block(k * CHUNK + j * BLOCK)

        send_prop(k).start()

    tiles = points // TILE

    @pl.loop(0, tiles)
    def _(t):
        lanes = pl.ds(pl.multiple_of(t * TILE, TILE), TILE)
        acc[:, lanes] = jnp.dot(parts[c], prop[:, lanes], preferred_element_type=jnp.float32)

    starts = list(range(0, bins, GROUP))
    for start in starts:
        size = min(GROUP, bins - start)

        @pl.loop(start // CHUNK, (start + size) // CHUNK)
        def _(k):
            send_prop(k).wait_recv()

        @pl.loop(0, tiles)
        def _(t):
            lanes = pl.ds(pl.multiple_of(t * TILE, TILE), TILE)
            total = acc[:, lanes] + jnp.dot(
                parts[1 - c, :, start:start + size], other[start:start + size, lanes],
                preferred_element_type=jnp.float32)
            if start != starts[-1]:
                acc[:, lanes] = total
            else:
                acc[bins:, lanes] = total[bins:]
                wet = flow[2:3, pl.ds(pl.multiple_of(wide_lanes + t * TILE, 128), TILE)]
                spec_v[:, lanes] = (
                    wet * jnp.maximum(prop[:, lanes].astype(jnp.float32) + total[:bins], 0.0)
                ).astype(jnp.bfloat16)
                pltpu.make_async_copy(spec_v.at[:, lanes], upd.at[:, lanes], out_sem.at[0, t]).start()
                pltpu.make_async_copy(
                    acc.at[pl.ds(bins, drift_rows), lanes], stk.at[:, lanes], out_sem.at[1, t]).start()

    for step in range(nw - 1):
        send_cur(step).wait_send()

    @pl.when(has_prev)
    def _():
        send_edge(True).wait_send()

        @pl.loop(0, chunks)
        def _(k):
            send_up(k).wait_send()

    @pl.when(has_next)
    def _():
        send_edge(False).wait_send()

        @pl.loop(0, chunks)
        def _(k):
            send_down(k).wait_send()

    @pl.loop(0, chunks)
    def _(k):
        send_prop(k).wait_send()

    @pl.loop(0, tiles)
    def _(t):
        lanes = pl.ds(pl.multiple_of(t * TILE, TILE), TILE)
        pltpu.make_async_copy(spec_v.at[:, lanes], upd.at[:, lanes], out_sem.at[0, t]).wait()
        pltpu.make_async_copy(
            acc.at[pl.ds(bins, drift_rows), lanes], stk.at[:, lanes], out_sem.at[1, t]).wait()


def kernel_device(counts, spectrum, wet_mask, currents, remap_index, remap_weights, source_matrix):
    ns, nw, nc = counts
    bins, points = spectrum.shape
    lat_rows, lon = wet_mask.shape
    rows = lat_rows // nw
    total = source_matrix.shape[1]
    drift_rows = 2 * LEVELS // nc
    chunks = bins // CHUNK
    tiles = points // TILE
    edge = SUBSTEPS * lon
    ext = points + 2 * edge
    hbm, vmem = pl.BlockSpec(memory_space=pl.ANY), pl.BlockSpec(memory_space=pltpu.VMEM)
    dma = pltpu.SemaphoreType.DMA
    bf16, f32 = jnp.bfloat16, jnp.float32
    updated, stokes = pl.pallas_call(
        functools.partial(wave_kernel, (ns, nw, nc, rows, lon)),
        out_shape=(
            jax.ShapeDtypeStruct((bins, points), bf16),
            jax.ShapeDtypeStruct((drift_rows, points), f32),
        ),
        in_specs=[hbm, vmem, vmem, hbm, hbm, hbm, hbm, hbm],
        out_specs=(hbm, hbm),
        scratch_shapes=[
            pltpu.VMEM((bins, points), bf16),
            pltpu.VMEM((bins, edge), bf16),
            pltpu.VMEM((bins, edge), bf16),
            pltpu.VMEM((bins, points), bf16),
            pltpu.VMEM((bins, points), bf16),
            pltpu.VMEM((bins + drift_rows, points), f32),
            pltpu.VMEM((bins + drift_rows, total), bf16),
            pltpu.VMEM((nc, bins + drift_rows, bins), bf16),
            pltpu.VMEM((2, bins, 128), f32),
            pltpu.VMEM((4, points), jnp.int32),
            pltpu.VMEM((4, points), f32),
            pltpu.VMEM((8, ext), f32),
            pltpu.VMEM((2, 8, 128), f32),
            pltpu.VMEM((8, 128), f32),
            pltpu.VMEM((nw, 8, 128), f32),
            pltpu.VMEM((2, BLOCK, ext), f32),
            pltpu.VMEM((5, BLOCK, ext), f32),
            dma((5,)), dma((chunks,)),
            dma((chunks,)), dma((chunks,)), dma((chunks,)), dma((chunks,)),
            dma((nw,)), dma((nw,)), dma((2,)), dma((2,)),
            dma((chunks,)), dma((chunks,)), dma((2, tiles)),
        ],
        compiler_params=pltpu.CompilerParams(
            collective_id=0, has_side_effects=True, vmem_limit_bytes=48 * 1024 * 1024
        ),
        name="wave_step",
    )(
        spectrum, wet_mask, currents, remap_index, remap_weights, source_matrix,
        jnp.asarray(speed_table(bins, total)), jnp.asarray(drift_table(total, nc)),
    )
    return updated, stokes.reshape(2, LEVELS // nc, points)


def per_device(counts, spectrum, wet_mask, currents, remap_index, remap_weights, source_matrix):
    ns, nw, nc = counts
    bins, points = spectrum.shape
    lat_rows, lon = wet_mask.shape
    rows = lat_rows // nw
    cells = currents.shape[1] * currents.shape[2]
    fits = (
        nc == 2 and nw > 1 and rows >= SUBSTEPS and lon == 256 and points % TILE == 0
        and bins % CHUNK == 0 and cells <= 128 and currents.shape[1] <= 8
        and bins // CHUNK >= AHEAD
    )
    if fits:
        return kernel_device(counts, spectrum, wet_mask, currents, remap_index, remap_weights, source_matrix)
    return plain_device(spectrum, wet_mask, currents, remap_index, remap_weights, source_matrix)


def solution(mesh):
    placed = (
        P("comp", ("strip", "wide")),
        P("strip", None),
        P(None, "strip", "wide"),
        P(None, "strip"),
        P(None, "strip"),
        P("comp", None),
    )
    counts = tuple(mesh.shape[axis] for axis in ("strip", "wide", "comp"))
    return jax.shard_map(
        functools.partial(per_device, counts),
        mesh=mesh,
        in_specs=placed,
        out_specs=(P("comp", ("strip", "wide")), P(None, "comp", ("strip", "wide"))),
        check_vma=False,
    )
```

```python
import functools
import math

import jax
import jax.numpy as jnp
import numpy as np
from jax import lax
from jax.experimental import pallas as pl
from jax.experimental.pallas import tpu as pltpu
from jax.sharding import PartitionSpec as P

NFREQ = 32
NDIR = 36
LEVELS = 32
SUBSTEPS = 4


courant = 0.45


def extended(cells, sides, width):
    for axis, dim in sides:
        count = lax.axis_size(axis)
        ends = count - 1
        head = lax.slice_in_dim(cells, 0, width, axis=dim)
        tail = lax.slice_in_dim(cells, cells.shape[dim] - width, cells.shape[dim], axis=dim)
        cells = jnp.concatenate(
            [
                lax.ppermute(tail, axis, [(i, (i + 1) % count) for i in range(ends)]),
                cells,
                lax.ppermute(head, axis, [((i + 1) % count, i) for i in range(ends)]),
            ],
            axis=dim,
        )
    return cells


def bin_speeds(first_bin, bin_count):
    index = first_bin + jnp.arange(bin_count, dtype=jnp.int32)
    freq_index = (index // NDIR).astype(jnp.float32)
    dir_index = (index % NDIR).astype(jnp.float32)
    group_speed = 0.35 + 0.65 * (NFREQ - 1 - freq_index) / (NFREQ - 1)
    heading = 2.0 * math.pi * (dir_index + 0.5) / NDIR
    return (
        (group_speed * jnp.cos(heading))[:, None, None],
        (group_speed * jnp.sin(heading))[:, None, None],
    )


def stokes_kernel(bin_count, first_level, level_count):
    index = jnp.arange(bin_count, dtype=jnp.int32)
    frequency = (index // NDIR + 1).astype(jnp.float32)
    heading = 2.0 * math.pi * ((index % NDIR).astype(jnp.float32) + 0.5) / NDIR
    level_index = (first_level + jnp.arange(level_count, dtype=jnp.int32)).astype(jnp.float32)
    damping = jnp.exp(-4.0 * frequency[None, :] * (level_index[:, None] + 0.5) / (NFREQ * LEVELS))
    amplitude = damping * (frequency / NFREQ)[None, :] / math.sqrt(NDIR)
    eastward = amplitude * jnp.cos(heading)[None, :]
    northward = amplitude * jnp.sin(heading)[None, :]
    return jnp.concatenate([eastward, northward], 0).astype(jnp.bfloat16)


def substep(energy, east_flow, north_flow, wet_frac, speed_east, speed_north):
    east_speed = speed_east + east_flow[None]
    north_speed = speed_north + north_flow[None]
    flux_lon = jnp.maximum(east_speed, 0.0) * energy + jnp.minimum(
        jnp.roll(east_speed, -1, 2), 0.0
    ) * jnp.roll(energy, -1, 2)
    flux_lat = (
        jnp.maximum(north_speed[:, :-1], 0.0) * energy[:, :-1]
        + jnp.minimum(north_speed[:, 1:], 0.0) * energy[:, 1:]
    )
    spread = flux_lon - jnp.roll(flux_lon, 1, 2)
    change = spread[:, 1:-1] + flux_lat[:, 1:] - flux_lat[:, :-1]
    return wet_frac[1:-1] * (energy[:, 1:-1] - courant * change)


def advance(widened, speed_east, speed_north):
    bin_share = speed_east.shape[0]
    energy = widened[:bin_share]
    east_flow = widened[bin_share]
    north_flow = widened[bin_share + 1]
    wet_frac = widened[bin_share + 2]
    energy = substep(energy, east_flow, north_flow, wet_frac, speed_east, speed_north)
    return energy


def interpolate(tiles, remap_index, remap_weights, lat_rows, lon_cells):
    ocean_rows = tiles.shape[1]
    ocean_cols = tiles.shape[2]
    block_points = 4 * lon_cells
    block_count = lat_rows // 4
    flow_table = tiles.reshape(2 * ocean_rows, ocean_cols)
    index_blocks = jnp.transpose(remap_index.reshape(4, block_count, block_points), (1, 0, 2))
    weight_blocks = jnp.transpose(remap_weights.reshape(4, block_count, block_points), (1, 0, 2))
    column_ids = jnp.arange(ocean_cols, dtype=jnp.int32)[None, :, None]
    row_ids = jnp.arange(ocean_rows, dtype=jnp.int32)[None, :, None]

    def one_block(inputs):
        cells, shares = inputs
        column_of = cells % ocean_cols
        row_of = cells // ocean_cols
        column_hot = (column_of[:, None, :] == column_ids).astype(jnp.float32)
        picked = jnp.einsum("mk,jkp->jmp", flow_table, column_hot, precision=lax.Precision.HIGHEST)
        picked = picked.reshape(4, 2, ocean_rows, block_points)
        row_weight = (row_of[:, None, :] == row_ids).astype(jnp.float32) * shares[:, None, :]
        return jnp.sum(picked * row_weight[:, None], (0, 2))

    blocks = lax.map(one_block, (index_blocks, weight_blocks))
    return jnp.transpose(blocks, (1, 0, 2)).reshape(2, lat_rows, lon_cells)


def plain_device(spectrum, wet_mask, currents, remap_index, remap_weights, source_matrix):
    wide_count = lax.axis_size("wide")
    wide_index = lax.axis_index("wide")
    comp_index = lax.axis_index("comp")
    lat_rows, lon_cells = wet_mask.shape
    local_bins, points = spectrum.shape
    tiles = lax.all_gather(currents, "wide", axis=2, tiled=True)
    surface = interpolate(tiles, remap_index, remap_weights, lat_rows, lon_cells)
    wet_frac = wet_mask.astype(jnp.float32)
    row_count = lat_rows // wide_count
    wet_rows = lax.dynamic_slice_in_dim(wet_frac, wide_index * row_count, row_count, 0)
    flow_rows = lax.dynamic_slice_in_dim(surface, wide_index * row_count, row_count, 1)
    speed_east, speed_north = bin_speeds(comp_index * local_bins, local_bins)
    energy = spectrum.astype(jnp.float32).reshape(local_bins, row_count, lon_cells) * wet_rows
    for repeat in range(SUBSTEPS):
        fields = jnp.concatenate([energy, flow_rows, wet_rows[None]], 0)
        widened = extended(fields, ((("strip", "wide"), 1),), 1)
        energy = advance(widened, speed_east, speed_north)
    returned = energy.astype(jnp.bfloat16).reshape(local_bins, points)
    level_rows = LEVELS // lax.axis_size("comp")
    first_level = comp_index * level_rows
    fragment = lax.all_gather(returned, "comp", axis=0, tiled=True)
    width = fragment.shape[0]
    kernel = stokes_kernel(width, first_level, level_rows)
    source_part = jnp.dot(source_matrix, fragment, preferred_element_type=jnp.float32)
    drift_part = jnp.dot(kernel, fragment, preferred_element_type=jnp.float32)
    wet_points = lax.dynamic_slice_in_dim(wet_frac.reshape(-1), wide_index * points, points, 0)
    updated = (
        wet_points[None, :] * jnp.maximum(returned.astype(jnp.float32) + source_part, 0.0)
    ).astype(jnp.bfloat16)
    return (updated, drift_part.reshape(2, level_rows, points))


CHUNK = 16
BLOCK = 16
FIRST = 2
AHEAD = 8
TILE = 512
GROUP = 256
MESH = pl.DeviceIdType.MESH


def speed_table(bin_count, bins_total):
    index = np.arange(bins_total)
    group_speed = 0.35 + 0.65 * (NFREQ - 1 - index // NDIR) / (NFREQ - 1)
    heading = 2.0 * math.pi * (index % NDIR + 0.5) / NDIR
    both = courant * np.stack([group_speed * np.cos(heading), group_speed * np.sin(heading)])
    return np.ascontiguousarray(np.broadcast_to(both[:, :, None], (2, bins_total, 128)).astype(np.float32))


def drift_table(bins_total, comp_count):
    index = np.arange(bins_total)
    frequency = (index // NDIR + 1).astype(np.float32)
    heading = 2.0 * math.pi * (index % NDIR + 0.5) / NDIR
    level = np.arange(LEVELS, dtype=np.float32)
    damping = np.exp(-4.0 * frequency[None, :] * (level[:, None] + 0.5) / (NFREQ * LEVELS))
    amplitude = damping * (frequency / NFREQ)[None, :] / math.sqrt(NDIR)
    both = np.stack([amplitude * np.cos(heading), amplitude * np.sin(heading)])
    both = both.reshape(2, comp_count, LEVELS // comp_count, bins_total)
    both = np.transpose(both, (1, 0, 2, 3)).reshape(comp_count, -1, bins_total)
    return both.astype(np.float32).astype(jnp.bfloat16)


def wave_kernel(
    sizes, spec, mask, cur, idx, wgt, src, speed, drift,
    upd, stk,
    spec_v, top, bot, prop, other, acc, src_v, parts, speed_v, idx_v, wgt_v, mask_v, cur_v,
    flow, cur_pad, cur_flat, curs, state, coef,
    load_sem, spec_sem, up_send, down_send, bot_recv, top_recv,
    cur_send, cur_recv, edge_send, edge_recv, prop_send, prop_recv, tail_send, tail_recv,
):
    ns, nw, nc, rows, lon = sizes
    bins, points = spec.shape
    depth = SUBSTEPS
    wide_lanes = depth * lon
    chunks = bins // CHUNK
    starts = list(range(0, bins, GROUP))
    whole = starts[-1] // CHUNK
    tiles = points // TILE
    drift_rows = drift.shape[1]
    ocean_cols, ocean_rows = cur.shape[1], cur.shape[2]
    s, w, c = lax.axis_index("strip"), lax.axis_index("wide"), lax.axis_index("comp")
    place = s * nw + w
    has_prev = place > 0
    has_next = place < ns * nw - 1
    before = jnp.maximum(place - 1, 0)
    after = jnp.minimum(place + 1, ns * nw - 1)
    prev_dev = (before // nw, before % nw, c)
    next_dev = (after // nw, after % nw, c)
    partner = (s, w, 1 - c)

    def span(k):
        return pl.ds(pl.multiple_of(k * CHUNK, CHUNK), CHUNK)

    own_rows = pl.ds(pl.multiple_of(c * bins, BLOCK), bins)
    own_points = pl.ds(pl.multiple_of(w * points, 128), points)
    loads = [
        pltpu.make_async_copy(cur, cur_v, load_sem.at[5]),
        pltpu.make_async_copy(mask, mask_v, load_sem.at[6]),
        pltpu.make_async_copy(idx.at[:, own_points], idx_v, load_sem.at[0]),
        pltpu.make_async_copy(wgt.at[:, own_points], wgt_v, load_sem.at[1]),
        pltpu.make_async_copy(speed.at[:, own_rows, :], speed_v, load_sem.at[2]),
        pltpu.make_async_copy(src, src_v.at[pl.ds(0, bins), :], load_sem.at[3]),
        pltpu.make_async_copy(drift.at[c], src_v.at[pl.ds(bins, drift_rows), :], load_sem.at[4]),
    ]

    def load_chunk(k):
        return pltpu.make_async_copy(spec.at[span(k), :], spec_v.at[span(k), :], spec_sem.at[k])

    def send_up(k):
        return pltpu.make_async_remote_copy(
            src_ref=spec.at[span(k), pl.ds(0, wide_lanes)], dst_ref=bot.at[span(k), :],
            send_sem=up_send.at[k], recv_sem=bot_recv.at[k], device_id=prev_dev, device_id_type=MESH)

    def send_down(k):
        return pltpu.make_async_remote_copy(
            src_ref=spec.at[span(k), pl.ds(points - wide_lanes, wide_lanes)], dst_ref=top.at[span(k), :],
            send_sem=down_send.at[k], recv_sem=top_recv.at[k], device_id=next_dev, device_id_type=MESH)

    def send_cur(step):
        return pltpu.make_async_remote_copy(
            src_ref=cur_flat, dst_ref=curs.at[w], send_sem=cur_send.at[step], recv_sem=cur_recv.at[step],
            device_id=(s, (w + step + 1) % nw, c), device_id_type=MESH)

    def take_cur(step):
        return pltpu.make_async_remote_copy(
            src_ref=cur_flat, dst_ref=curs.at[(w + nw - step - 1) % nw], send_sem=cur_send.at[step],
            recv_sem=cur_recv.at[step], device_id=(s, (w + step + 1) % nw, c), device_id_type=MESH)

    def send_edge(up):
        if up:
            return pltpu.make_async_remote_copy(
                src_ref=flow.at[:, pl.ds(wide_lanes, wide_lanes)],
                dst_ref=flow.at[:, pl.ds(wide_lanes + points, wide_lanes)],
                send_sem=edge_send.at[0], recv_sem=edge_recv.at[0], device_id=prev_dev, device_id_type=MESH)
        return pltpu.make_async_remote_copy(
            src_ref=flow.at[:, pl.ds(points, wide_lanes)], dst_ref=flow.at[:, pl.ds(0, wide_lanes)],
            send_sem=edge_send.at[1], recv_sem=edge_recv.at[1], device_id=next_dev, device_id_type=MESH)

    def send_prop(k):
        return pltpu.make_async_remote_copy(
            src_ref=prop.at[span(k), :], dst_ref=other.at[span(k), :],
            send_sem=prop_send.at[k], recv_sem=prop_recv.at[k], device_id=partner, device_id_type=MESH)

    def send_tail(t):
        piece = (pl.ds(starts[-1], bins - starts[-1]), pl.ds(pl.multiple_of(t * TILE, TILE), TILE))
        return pltpu.make_async_remote_copy(
            src_ref=prop.at[piece], dst_ref=other.at[piece],
            send_sem=tail_send.at[t], recv_sem=tail_recv.at[t], device_id=partner, device_id_type=MESH)

    for copy in loads[:4]:
        copy.start()
    flow[...] = jnp.zeros_like(flow)

    @pl.when(jnp.logical_not(has_prev))
    def _():
        top[...] = jnp.zeros_like(top)

    @pl.when(jnp.logical_not(has_next))
    def _():
        bot[...] = jnp.zeros_like(bot)

    barrier = pltpu.get_barrier_semaphore()
    for step in range(1, nw):
        pl.semaphore_signal(barrier, inc=1, device_id=(s, (w + step) % nw, c), device_id_type=MESH)
    pl.semaphore_signal(barrier, inc=1, device_id=partner, device_id_type=MESH)
    cross_prev = jnp.logical_and(has_prev, w == 0)
    cross_next = jnp.logical_and(has_next, w == nw - 1)

    @pl.when(cross_prev)
    def _():
        pl.semaphore_signal(barrier, inc=1, device_id=prev_dev, device_id_type=MESH)

    @pl.when(cross_next)
    def _():
        pl.semaphore_signal(barrier, inc=1, device_id=next_dev, device_id_type=MESH)

    @pl.loop(0, chunks)
    def _(k):
        load_chunk(k).start()

    for copy in loads[4:]:
        copy.start()
    cur_pad[...] = jnp.zeros_like(cur_pad)
    loads[0].wait()
    cur_flat[...] = jnp.zeros_like(cur_flat)
    for comp in range(2):
        cur_pad[comp, 0:ocean_cols, 0:ocean_rows] = cur_v[comp]
        line = cur_pad[comp, 0:1, :]
        for col in range(1, ocean_cols):
            line = line + pltpu.roll(cur_pad[comp, col:col + 1, :], col * ocean_rows, 1)
        cur_flat[comp:comp + 1, :] = line
    curs[w] = cur_flat[...]

    pl.semaphore_wait(barrier, nw + cross_prev.astype(jnp.int32) + cross_next.astype(jnp.int32))

    for step in range(nw - 1):
        send_cur(step).start()

    def start_halo(k):
        @pl.when(has_prev)
        def _():
            send_up(k).start()

        @pl.when(has_next)
        def _():
            send_down(k).start()

    @pl.loop(0, FIRST)
    def _(k):
        start_halo(k)

    for copy in loads[1:4]:
        copy.wait()
    for row in range(rows):
        lanes = slice(wide_lanes + row * lon, wide_lanes + (row + 1) * lon)
        flow[2:3, lanes] = mask_v[pl.ds(w * rows + row, 1), :].astype(jnp.float32)
    for step in range(nw - 1):
        take_cur(step).wait_recv()
    total_cols = ocean_cols * nw
    for piece in range(points // 256):
        lanes = [slice(piece * 256 + h * 128, piece * 256 + (h + 1) * 128) for h in range(2)]
        cells = jnp.concatenate([idx_v[:, part] for part in lanes], 0)
        shares = jnp.concatenate([wgt_v[:, part] for part in lanes], 0)
        row_of, col_of = cells // total_cols, cells % total_cols
        tile_of = col_of // ocean_cols
        spot = col_of % ocean_cols * ocean_rows + row_of
        for comp in range(2):
            picked = jnp.zeros(cells.shape, jnp.float32)
            for tile in range(nw):
                table = jnp.broadcast_to(curs[tile, comp:comp + 1, :], cells.shape)
                found = jnp.take_along_axis(table, spot, axis=1, mode="promise_in_bounds")
                picked = jnp.where(tile_of == tile, found, picked)
            picked = courant * picked * shares
            for h in range(2):
                flow[comp:comp + 1, wide_lanes + piece * 256 + h * 128:wide_lanes + piece * 256 + (h + 1) * 128] = (
                    jnp.sum(picked[4 * h:4 * h + 4], 0, keepdims=True))

    @pl.when(has_prev)
    def _():
        send_edge(True).start()

    @pl.when(has_next)
    def _():
        send_edge(False).start()

    @pl.loop(FIRST, AHEAD)
    def _(k):
        start_halo(k)

    loads[4].wait()

    @pl.when(has_next)
    def _():
        send_edge(True).wait_recv()

    @pl.when(has_prev)
    def _():
        send_edge(False).wait_recv()

    ext = rows + 2 * depth

    def at(row):
        return slice(row * lon, (row + 1) * lon)

    def block(first):
        here = pl.ds(pl.multiple_of(first, BLOCK), BLOCK)
        cx = jnp.concatenate([speed_v[0, here, :]] * (lon // 128), 1)
        cy = jnp.concatenate([speed_v[1, here, :]] * (lon // 128), 1)
        for row in range(ext):
            if row < depth:
                cells = top[here, at(row)]
            elif row < depth + rows:
                cells = spec_v[here, at(row - depth)]
            else:
                cells = bot[here, at(row - depth - rows)]
            state[0, :, at(row)] = cells.astype(jnp.float32) * flow[2:3, at(row)]

        def north(row):
            speed_n = cy + flow[1:2, at(row)]
            up = jnp.maximum(speed_n, 0.0)
            return up, up - speed_n

        below, mid = north(0), north(1)
        for row in range(1, ext - 1):
            above = north(row + 1)
            speed_e = cx + flow[0:1, at(row)]
            east = jnp.maximum(speed_e, 0.0)
            west = east - speed_e
            wet = flow[2:3, at(row)]
            coef[0, :, at(row)] = wet * (1.0 - (east + west) - (mid[0] + mid[1]))
            coef[1, :, at(row)] = wet * pltpu.roll(east, 1, 1)
            coef[2, :, at(row)] = wet * pltpu.roll(west, lon - 1, 1)
            coef[3, :, at(row)] = wet * below[0]
            coef[4, :, at(row)] = wet * above[1]
            below, mid = mid, above
        for repeat in range(depth):
            now, later = repeat % 2, (repeat + 1) % 2
            low, mid_e = state[now, :, at(repeat)], state[now, :, at(repeat + 1)]
            for row in range(repeat + 1, ext - 1 - repeat):
                high = state[now, :, at(row + 1)]
                result = (
                    (coef[0, :, at(row)] * mid_e
                     + (coef[1, :, at(row)] * pltpu.roll(mid_e, 1, 1)
                        + coef[2, :, at(row)] * pltpu.roll(mid_e, lon - 1, 1)))
                    + (coef[3, :, at(row)] * low + coef[4, :, at(row)] * high))
                if repeat < depth - 1:
                    state[later, :, at(row)] = result
                else:
                    prop[here, at(row - depth)] = result.astype(jnp.bfloat16)
                low, mid_e = mid_e, high

    @pl.loop(0, chunks)
    def _(k):
        load_chunk(k).wait()

        @pl.when(has_next)
        def _():
            send_up(k).wait_recv()

        @pl.when(has_prev)
        def _():
            send_down(k).wait_recv()

        @pl.when(k + AHEAD < chunks)
        def _():
            start_halo(k + AHEAD)

        block(k * CHUNK)

        @pl.when(k < whole)
        def _():
            send_prop(k).start()

    @pl.loop(0, tiles)
    def _(t):
        send_tail(t).start()

    for copy in loads[5:]:
        copy.wait()
    for half in range(nc):
        parts[half] = src_v[:, half * bins:(half + 1) * bins]

    @pl.loop(0, tiles)
    def _(t):
        lanes = pl.ds(pl.multiple_of(t * TILE, TILE), TILE)
        acc[:, lanes] = jnp.dot(parts[c], prop[:, lanes], preferred_element_type=jnp.float32)

    for start in starts:
        size = min(GROUP, bins - start)

        if start != starts[-1]:
            @pl.loop(start // CHUNK, (start + size) // CHUNK)
            def _(k):
                send_prop(k).wait_recv()

        @pl.loop(0, tiles)
        def _(t):
            if start == starts[-1]:
                send_tail(t).wait_recv()
            lanes = pl.ds(pl.multiple_of(t * TILE, TILE), TILE)
            total = acc[:, lanes] + jnp.dot(
                parts[1 - c, :, start:start + size], other[start:start + size, lanes],
                preferred_element_type=jnp.float32)
            if start != starts[-1]:
                acc[:, lanes] = total
            else:
                stk[:, lanes] = total[bins:]
                wet = flow[2:3, pl.ds(pl.multiple_of(wide_lanes + t * TILE, 128), TILE)]
                upd[:, lanes] = (
                    wet * jnp.maximum(prop[:, lanes].astype(jnp.float32) + total[:bins], 0.0)
                ).astype(jnp.bfloat16)

    for step in range(nw - 1):
        send_cur(step).wait_send()

    @pl.when(has_prev)
    def _():
        send_edge(True).wait_send()

        @pl.loop(0, chunks)
        def _(k):
            send_up(k).wait_send()

    @pl.when(has_next)
    def _():
        send_edge(False).wait_send()

        @pl.loop(0, chunks)
        def _(k):
            send_down(k).wait_send()

    @pl.loop(0, whole)
    def _(k):
        send_prop(k).wait_send()

    @pl.loop(0, tiles)
    def _(t):
        send_tail(t).wait_send()


def kernel_device(counts, spectrum, wet_mask, currents, remap_index, remap_weights, source_matrix):
    ns, nw, nc = counts
    bins, points = spectrum.shape
    lat_rows, lon = wet_mask.shape
    rows = lat_rows // nw
    total = source_matrix.shape[1]
    drift_rows = 2 * LEVELS // nc
    chunks = bins // CHUNK
    tiles = points // TILE
    edge = SUBSTEPS * lon
    ext = points + 2 * edge
    hbm, vmem = pl.BlockSpec(memory_space=pltpu.HBM), pl.BlockSpec(memory_space=pltpu.VMEM)
    dma = pltpu.SemaphoreType.DMA
    bf16, f32 = jnp.bfloat16, jnp.float32
    updated, stokes = pl.pallas_call(
        functools.partial(wave_kernel, (ns, nw, nc, rows, lon)),
        out_shape=(
            pltpu.VMEM((bins, points), bf16),
            pltpu.VMEM((drift_rows, points), f32),
        ),
        in_specs=[hbm] * 8,
        out_specs=(vmem, vmem),
        scratch_shapes=[
            pltpu.VMEM((bins, points), bf16),
            pltpu.VMEM((bins, edge), bf16),
            pltpu.VMEM((bins, edge), bf16),
            pltpu.VMEM((bins, points), bf16),
            pltpu.VMEM((bins, points), bf16),
            pltpu.VMEM((bins + drift_rows, points), f32),
            pltpu.VMEM((bins + drift_rows, total), bf16),
            pltpu.VMEM((nc, bins + drift_rows, bins), bf16),
            pltpu.VMEM((2, bins, 128), f32),
            pltpu.VMEM((4, points), jnp.int32),
            pltpu.VMEM((4, points), f32),
            pltpu.VMEM(wet_mask.shape, jnp.int32),
            pltpu.VMEM((2, currents.shape[2], currents.shape[1]), f32),
            pltpu.VMEM((8, ext), f32),
            pltpu.VMEM((2, 8, 128), f32),
            pltpu.VMEM((8, 128), f32),
            pltpu.VMEM((nw, 8, 128), f32),
            pltpu.VMEM((2, BLOCK, ext), f32),
            pltpu.VMEM((5, BLOCK, ext), f32),
            dma((7,)), dma((chunks,)),
            dma((chunks,)), dma((chunks,)), dma((chunks,)), dma((chunks,)),
            dma((nw,)), dma((nw,)), dma((2,)), dma((2,)),
            dma((chunks,)), dma((chunks,)), dma((tiles,)), dma((tiles,)),
        ],
        compiler_params=pltpu.CompilerParams(
            collective_id=0, has_side_effects=True, vmem_limit_bytes=48 * 1024 * 1024
        ),
        name="wave_step",
    )(*(pltpu.with_memory_space_constraint(array, pltpu.HBM) for array in (
        spectrum, wet_mask, jnp.transpose(currents, (0, 2, 1)), remap_index, remap_weights, source_matrix,
        jnp.asarray(speed_table(bins, total)), jnp.asarray(drift_table(total, nc)),
    )))
    return updated, stokes.reshape(2, LEVELS // nc, points)


def per_device(counts, spectrum, wet_mask, currents, remap_index, remap_weights, source_matrix):
    ns, nw, nc = counts
    bins, points = spectrum.shape
    lat_rows, lon = wet_mask.shape
    rows = lat_rows // nw
    cells = currents.shape[1] * currents.shape[2]
    fits = (
        nc == 2 and nw > 1 and rows >= SUBSTEPS and lon == 256 and points % TILE == 0
        and bins % CHUNK == 0 and cells <= 128 and currents.shape[2] <= 8 and currents.shape[1] <= 128
        and bins // CHUNK >= AHEAD
    )
    if fits:
        return kernel_device(counts, spectrum, wet_mask, currents, remap_index, remap_weights, source_matrix)
    return plain_device(spectrum, wet_mask, currents, remap_index, remap_weights, source_matrix)


def solution(mesh):
    placed = (
        P("comp", ("strip", "wide")),
        P("strip", None),
        P(None, "strip", "wide"),
        P(None, "strip"),
        P(None, "strip"),
        P("comp", None),
    )
    counts = tuple(mesh.shape[axis] for axis in ("strip", "wide", "comp"))
    return jax.shard_map(
        functools.partial(per_device, counts),
        mesh=mesh,
        in_specs=placed,
        out_specs=(P("comp", ("strip", "wide")), P(None, "comp", ("strip", "wide"))),
        check_vma=False,
    )
```
